32 devices in a mesh: mp: 2 (over x), latent: 16 (over z, y, core).
Axes of the slice: x: 2, y: 2, z: 4, core: 2. Of those that a mesh axis runs over, the one named last changes fastest.
Arguments:
- resid_in: bfloat16 [512, 4096], P('latent', 'mp'), may hold values from -160 to 160
- cotangent: bfloat16 [512, 4096], P('latent', 'mp'), may hold values from -0.29882812 to 0.29882812
- norm1_gain: float32 [4096], P('mp'), may hold values from 0.1 to 1.9
- gate1: bfloat16 [4096, 14336], P('mp', 'latent'), may hold values from -0.09375 to 0.09375
- up1: bfloat16 [4096, 14336], P('mp', 'latent'), may hold values from -0.09375 to 0.09375
- down1: bfloat16 [14336, 4096], P('latent', 'mp'), may hold values from -0.046875 to 0.046875
- enc_weight: bfloat16 [4096, 32768], P('mp', 'latent'), may hold values from -0.09375 to 0.09375
- enc_bias: float32 [32768], P('latent'), may hold values from -3 to 3
- dec_weight: bfloat16 [32768, 4096], P('latent', 'mp'), may hold values from -0.03125 to 0.03125
- dec_bias: float32 [4096], P('mp'), may hold values from -3 to 3
- norm2_gain: float32 [4096], P('mp'), may hold values from 0.25 to 6
- gate2: bfloat16 [4096, 14336], P('mp', 'latent'), may hold values from -0.09375 to 0.09375
- up2: bfloat16 [4096, 14336], P('mp', 'latent'), may hold values from -0.09375 to 0.09375
- down2: bfloat16 [14336, 4096], P('latent', 'mp'), may hold values from -0.046875 to 0.046875
Outputs:
- enc_grad: float32 [4096, 32768], P('mp', 'latent')
- dec_grad: float32 [32768, 4096], P('latent', 'mp')
The draws below stay inside these ranges and needn't reach their ends.
All inputs are finite; a program needn't handle non-finite values.
Results may differ from the reference program's by a relative error of at most 0.025.
Values may be sent and summed in bfloat16 or wider, within the bound.
No kernel may reach another device: no remote copies, remote signals or barrier semaphores. Data moves between devices by JAX's collectives and lax.ppermute only.
A program may use at most 128 MiB of HBM per device.

```python
import jax
import jax.numpy as jnp
from jax import lax

D = 4096
FF = 14336
L = 32768
TOK = 512


def draw_resid_in(key, part):
    keys = jax.random.split(key, 3)
    base = jnp.clip(jax.random.normal(keys[0], (TOK, D), jnp.float32), -6.0, 6.0)
    ladder = jnp.arange(D).astype(jnp.float32) / D - 0.5
    columns = 10.0 ** ladder * jnp.exp(0.3 * jax.random.uniform(keys[1], (D,), jnp.float32))
    rows = 10.0 ** (jax.random.uniform(keys[2], (TOK, 1), jnp.float32) - 0.5)
    return (base * columns * rows).astype(jnp.bfloat16)


def draw_norm2_gain(key, part):
    keys = jax.random.split(jax.random.fold_in(key, 71), 1)
    ladder = jnp.arange(D).astype(jnp.float32) / D
    jitter = jax.random.uniform(keys[0], (D,), jnp.float32)
    values = 0.4 * 10.0 ** ladder * jnp.exp(0.2 * jitter)
    return jnp.clip(values, 0.25, 6.0).astype(jnp.float32)


def level_of(own_key, extent, shards, smallest, top_value):
    def one(dim, parts):
        heights = jax.random.uniform(jax.random.fold_in(jax.random.fold_in(own_key, 6), dim), (parts,), jnp.float32, smallest / len(shards), top_value / len(shards))
        return jnp.repeat(jnp.exp(heights), extent[dim] // parts).reshape((-1,) + (1,) * (len(extent) - dim - 1))

    loudness = one(*shards[0])
    for cut in shards[1:]:
        loudness = loudness * one(*cut)
    return loudness


def normal_values(key, dims, scale, reach, pieces=(), dtype=jnp.bfloat16):
    loudness = level_of(key, dims, pieces, -0.22, 0.18) if pieces else 1.0
    drawn = jax.random.normal(key, dims, jnp.float32) * scale * loudness
    return jnp.minimum(jnp.maximum(drawn, -reach), reach).astype(dtype)


def setup_inputs(seed: int = 0) -> dict:
    seeds = jax.random.split(jax.random.key(seed), 15)
    return {
        "resid_in": draw_resid_in(jax.random.fold_in(seeds[14], 71), 0),
        "cotangent": normal_values(seeds[1], (TOK, D), 0.05, 0.29882812, ((0, 16), (1, 2))),
        "norm1_gain": jnp.clip(1.0 + 0.18 * jax.random.normal(seeds[2], (D,), jnp.float32), 0.1, 1.9),
        "gate1": normal_values(seeds[3], (D, FF), D ** -0.5, 0.09375, ((0, 2), (1, 16))),
        "up1": normal_values(seeds[4], (D, FF), D ** -0.5, 0.09375, ((0, 2), (1, 16))),
        "down1": normal_values(seeds[5], (FF, D), FF ** -0.5, 0.046875, ((0, 16), (1, 2))),
        "enc_weight": normal_values(seeds[6], (D, L), D ** -0.5, 0.09375, ((0, 2), (1, 16))),
        "enc_bias": normal_values(seeds[7], (L,), 0.5, 3.0, ((0, 16),), jnp.float32),
        "dec_weight": normal_values(seeds[8], (L, D), L ** -0.5, 0.03125, ((0, 16), (1, 2))),
        "dec_bias": normal_values(seeds[9], (D,), 0.5, 3.0, ((0, 2),), jnp.float32),
        "norm2_gain": draw_norm2_gain(jax.random.fold_in(seeds[14], 71), 0),
        "gate2": normal_values(seeds[11], (D, FF), D ** -0.5, 0.09375, ((0, 2), (1, 16))),
        "up2": normal_values(seeds[12], (D, FF), D ** -0.5, 0.09375, ((0, 2), (1, 16))),
        "down2": normal_values(seeds[13], (FF, D), FF ** -0.5, 0.046875, ((0, 16), (1, 2))),
    }


def inverse_rms(values):
    return lax.rsqrt(lax.optimization_barrier(jnp.mean(values * values, axis=1, keepdims=True)) + 1e-05)

def matmul(left, right):
    return jnp.dot(left, right, preferred_element_type=jnp.float32)

def contract(left, right, left_dim, right_dim):
    return lax.dot_general(left, right, (((left_dim,), (right_dim,)), ((), ())), preferred_element_type=jnp.float32)

def reference(resid_in, cotangent, norm1_gain, gate1, up1, down1, enc_weight, enc_bias, dec_weight, dec_bias, norm2_gain, gate2, up2, down2):
    resid = resid_in.astype(jnp.float32)
    inv_first = inverse_rms(resid)
    normed_first = (resid * inv_first * norm1_gain).astype(jnp.bfloat16)
    gate_first = matmul(normed_first, gate1)
    up_first = matmul(normed_first, up1)
    hidden_first = (jax.nn.silu(gate_first) * up_first).astype(jnp.bfloat16)
    block_out = (resid + matmul(hidden_first, down1)).astype(jnp.bfloat16)
    centered = (block_out.astype(jnp.float32) - dec_bias).astype(jnp.bfloat16)
    preact = matmul(centered, enc_weight) + enc_bias
    codes = (jax.nn.softplus(4.0 * preact) / 4.0).astype(jnp.bfloat16)
    recon = (matmul(codes, dec_weight) + dec_bias).astype(jnp.bfloat16)
    recon_f = recon.astype(jnp.float32)
    inv_second = inverse_rms(recon_f)
    normed_second = (recon_f * inv_second * norm2_gain).astype(jnp.bfloat16)
    gate_second = matmul(normed_second, gate2)
    up_second = matmul(normed_second, up2)
    hidden_grad = contract(cotangent, down2, 1, 1)
    squash = jax.nn.sigmoid(gate_second)
    gate_grad = (hidden_grad * up_second * squash * (1.0 + gate_second * (1.0 - squash))).astype(jnp.bfloat16)
    up_grad = (hidden_grad * gate_second * squash).astype(jnp.bfloat16)
    normed_grad = contract(gate_grad, gate2, 1, 1) + contract(up_grad, up2, 1, 1)
    scaled = normed_grad * norm2_gain
    inner = lax.optimization_barrier(jnp.mean(scaled * recon_f, axis=1, keepdims=True))
    recon_grad = (cotangent.astype(jnp.float32) + scaled * inv_second - recon_f * inv_second ** 3 * inner).astype(jnp.bfloat16)
    dec_grad = contract(codes, recon_grad, 0, 0)
    codes_grad = contract(recon_grad, dec_weight, 1, 1)
    preact_grad = (codes_grad * jax.nn.sigmoid(4.0 * preact)).astype(jnp.bfloat16)
    enc_grad = contract(centered, preact_grad, 0, 0)
    return (enc_grad, dec_grad)
```

```python
import jax
import jax.numpy as jnp
from jax import lax
from jax.sharding import PartitionSpec as P

CHUNKS = 2


def matmul(left, right):
    return jnp.dot(left, right, preferred_element_type=jnp.float32)


def contract(left, right, left_dim, right_dim):
    return lax.dot_general(
        left, right, (((left_dim,), (right_dim,)), ((), ())), preferred_element_type=jnp.float32
    )


def narrow(values):
    return values.astype(jnp.bfloat16)


def wide(values):
    return values.astype(jnp.float32)


def swap(values, axis, size, mask):
    return lax.ppermute(values, axis, [(i, i ^ mask) for i in range(size)])


def make_step(mp, latent):
    chips = latent // 2
    line_size = min(4, chips)
    row = chips // line_size
    line_bits = line_size.bit_length() - 1

    def gather_line(block):
        spot = (lax.axis_index("latent") // (2 * row)) % line_size
        out = block
        for bit in range(line_bits):
            other = swap(out, "latent", latent, 2 * row << bit)
            low = (spot >> bit) % 2 == 0
            out = jnp.concatenate(
                [jnp.where(low, out, other), jnp.where(low, other, out)], axis=0
            )
        return out

    def sum_line(values):
        for bit in range(line_bits):
            sent = narrow(values)
            values = wide(sent) + wide(swap(sent, "latent", latent, 2 * row << bit))
        return values

    def spread(line):
        plane = [line] + [swap(line, "latent", latent, 2 * k) for k in range(1, row)]
        near = jnp.concatenate(plane, axis=0)
        return jnp.concatenate([near, swap(near, "latent", latent, 1)], axis=0)

    def collect(partial):
        half = partial.shape[0] // 2
        near = partial[:half] + wide(swap(narrow(partial[half:]), "latent", latent, 1))
        size = half // row
        line = near[:size]
        for k in range(1, row):
            line = line + wide(swap(narrow(near[k * size : (k + 1) * size]), "latent", latent, 2 * k))
        return sum_line(line)

    def after(values, token):
        width = values.shape[1] if values.shape[1] <= token.shape[1] else 1
        edge = token[:1, :width]
        return jnp.where(edge == edge, values, jnp.zeros_like(values))

    def total_exact(values):
        if mp == 2:
            return values + swap(values, "mp", mp, 1)
        return lax.psum(values, "mp")

    def on_device(
        resid_in,
        cotangent,
        norm1_gain,
        gate1,
        up1,
        down1,
        enc_weight,
        enc_bias,
        dec_weight,
        dec_bias,
        norm2_gain,
        gate2,
        up2,
        down2,
    ):
        eps = 1e-05
        width = resid_in.shape[1] * mp
        rows = resid_in.shape[0] // CHUNKS
        ranges = [slice(i * rows, (i + 1) * rows) for i in range(CHUNKS)]

        def inverse_rms(values):
            values = wide(values)
            squares = jnp.sum(values * values, axis=1, keepdims=True)
            return lax.rsqrt(total_exact(squares) / width + eps)

        def first_sums(stream):
            scaled = narrow(wide(stream) * norm1_gain)
            inv = inverse_rms(stream)
            return matmul(scaled, gate1), matmul(scaled, up1), inv

        def first_hidden(gate, up, inv):
            return narrow(jax.nn.silu(gate * inv) * (up * inv))

        def first_out(resid, partial):
            block_out = narrow(wide(resid) + collect(partial))
            return narrow(wide(block_out) - dec_bias)

        def encode(preact):
            slope = jax.nn.sigmoid(4.0 * preact)
            codes = narrow(jax.nn.softplus(4.0 * preact) / 4.0)
            return slope, codes

        def second_sums(recon):
            inv = inverse_rms(recon)
            scaled = narrow(wide(recon) * norm2_gain)
            return matmul(scaled, gate2), matmul(scaled, up2), inv

        def second_grads(hidden_grad, gate, up):
            squash = jax.nn.sigmoid(gate)
            gate_grad = narrow(hidden_grad * up * squash * (1.0 + gate * (1.0 - squash)))
            up_grad = narrow(hidden_grad * gate * squash)
            return gate_grad, up_grad

        def second_out(recon, cot, partial, inv):
            normed_grad = collect(partial)
            scaled_grad = normed_grad * norm2_gain
            recon_f = wide(recon)
            inner = total_exact(jnp.sum(scaled_grad * recon_f, axis=1, keepdims=True)) / width
            inv = inv[: recon.shape[0]]
            return narrow(wide(cot) + scaled_grad * inv - recon_f * inv**3 * inner)

        turn = [None]

        def send(partial):
            if mp == 2:
                return partial, swap(narrow(partial), "mp", mp, 1)
            return partial, lax.psum(partial, "mp") - partial

        def arrive(pair):
            mine, others = pair
            return mine + wide(others if turn[0] is None else after(others, turn[0]))

        each = range(CHUNKS)
        both = jnp.split(gather_line(cotangent).reshape(-1, CHUNKS, rows, cotangent.shape[1]), CHUNKS, 1)
        cots = [cot.reshape(-1, cotangent.shape[1]) for cot in both]
        resids, firsts, centereds, preacts, hidden_grads, middles, seconds, recon_grads, last = (
            [] for _ in range(9)
        )
        for i in each:
            block = resid_in[ranges[i]]
            resid = gather_line(block if i == 0 else after(block, turn[0]))
            turn[0] = resid
            resids.append(resid)
            gate, up, inv = first_sums(spread(resid))
            firsts.append((send(gate), send(up), inv))
        for i in each:
            gate, up, inv = firsts[i]
            hidden = first_hidden(arrive(gate), arrive(up), inv)
            home = first_out(resids[i], matmul(hidden, down1))
            turn[0] = home
            centered, cot_all = jnp.split(spread(jnp.concatenate([home, cots[i]], axis=1)), 2, axis=1)
            centereds.append(centered)
            preacts.append(send(matmul(centered, enc_weight)))
            hidden_grads.append(send(contract(cot_all, down2, 1, 1)))
        for i in each:
            slope, codes = encode(arrive(preacts[i]) + enc_bias)
            recon = narrow(collect(matmul(codes, dec_weight)) + dec_bias)
            turn[0] = recon
            middles.append((slope, codes, recon))
            gate, up, inv = second_sums(spread(recon))
            seconds.append((send(gate), send(up), inv))
        for i in each:
            gate, up, inv = seconds[i]
            gate_grad, up_grad = second_grads(
                arrive(hidden_grads[i]), arrive(gate) * inv, arrive(up) * inv
            )
            partial = contract(gate_grad, gate2, 1, 1) + contract(up_grad, up2, 1, 1)
            home = second_out(middles[i][2], cots[i], partial, inv)
            turn[0] = home
            recon_grad = spread(home)
            recon_grads.append(recon_grad)
            last.append(send(contract(recon_grad, dec_weight, 1, 1)))
        preact_grads = [narrow(arrive(item) * middle[0]) for item, middle in zip(last, middles)]
        codes = jnp.concatenate([middle[1] for middle in middles], axis=0)
        centered = jnp.concatenate(centereds, axis=0)
        dec_grad = contract(codes, jnp.concatenate(recon_grads, axis=0), 0, 0)
        enc_grad = contract(centered, jnp.concatenate(preact_grads, axis=0), 0, 0)
        return (enc_grad, dec_grad)

    return on_device


def solution(mesh):
    in_specs = (
        P("latent", "mp"),
        P("latent", "mp"),
        P("mp"),
        P("mp", "latent"),
        P("mp", "latent"),
        P("latent", "mp"),
        P("mp", "latent"),
        P("latent"),
        P("latent", "mp"),
        P("mp"),
        P("mp"),
        P("mp", "latent"),
        P("mp", "latent"),
        P("latent", "mp"),
    )
    out_specs = (P("mp", "latent"), P("latent", "mp"))
    step = make_step(mesh.shape["mp"], mesh.shape["latent"])
    return jax.shard_map(step, mesh=mesh, in_specs=in_specs, out_specs=out_specs, check_vma=False)
```

```python
import jax
import jax.numpy as jnp
from jax import lax
from jax.sharding import PartitionSpec as P

CHUNKS = 2
ORDER = (
    ("aaacaca" + "bbbb")
    + ("abaacaa" + "bacbabcbb")
    + ("ababacaa" + "bababbb")
    + ("ababaaa" + "bababbb")
    + ("bb" + "ab")
)
FIRST_PIECE = 4


def matmul(left, right):
    return jnp.dot(left, right, preferred_element_type=jnp.float32)


def contract(left, right, left_dim, right_dim):
    return lax.dot_general(
        left, right, (((left_dim,), (right_dim,)), ((), ())), preferred_element_type=jnp.float32
    )


def narrow(values):
    return values.astype(jnp.bfloat16)


def wide(values):
    return values.astype(jnp.float32)


def swap(values, axis, size, mask):
    return lax.ppermute(values, axis, [(i, i ^ mask) for i in range(size)])


def after(values, token):
    width = values.shape[1]
    if token is None or width == 1:
        return values
    pieces = -(-width // token.shape[1])
    edge = jnp.concatenate([token[k : k + 1] for k in range(pieces)], axis=1)[:, :width]
    return jnp.where(edge == edge, values, jnp.zeros_like(values))


class Traffic:
    def __init__(self):
        self.token = None
        self.pending = []

    def post(self, values, axis, size, mask):
        self.token = values
        return swap(values, axis, size, mask)

    def post_sum(self, values, size):
        got = self.post(values, "mp", size, 1)
        self.pending.append(got)
        return got

    def meet(self, values, count=1):
        for got in self.pending[:count]:
            values = after(values, got)
        self.pending = self.pending[count:]
        return values

    def run(self, generators, order):
        held, results = {}, {}
        for name in order:
            values = held.get(name)
            if values is not None:
                values = [after(got, self.token) for got in values]
            try:
                held[name] = generators[name].send(values)
            except StopIteration as end:
                results[name] = end.value
        return results


def make_step(mp, latent):
    chips = latent // 2
    line_size = min(4, chips)
    row = chips // line_size
    line_bits = line_size.bit_length() - 1

    def on_device(
        resid_in,
        cotangent,
        norm1_gain,
        gate1,
        up1,
        down1,
        enc_weight,
        enc_bias,
        dec_weight,
        dec_bias,
        norm2_gain,
        gate2,
        up2,
        down2,
    ):
        eps = 1e-05
        width = resid_in.shape[1] * mp
        rows = resid_in.shape[0] // CHUNKS
        traffic = Traffic()

        def product(left, right, right_dim=0):
            return contract(left, right, 1, right_dim)

        def post_line(values, bit):
            return traffic.post(values, "latent", latent, 2 * row << bit)

        def post_plane(values, k):
            return traffic.post(values, "latent", latent, 2 * k)

        def post_core(values):
            return traffic.post(values, "latent", latent, 1)

        def post_sum(partial, exact=False):
            if mp != 2:
                return lax.psum(partial, "mp") - partial
            if exact:
                return swap(partial, "mp", mp, 1)
            return traffic.post_sum(narrow(partial), mp)

        def post_pieces(partial):
            first = partial.shape[0] // FIRST_PIECE
            return [post_sum(partial[:first]), post_sum(partial[first:])]

        def gather_line(block):
            spot = (lax.axis_index("latent") // (2 * row)) % line_size
            for bit in range(line_bits):
                (other,) = yield [post_line(block, bit)]
                low = (spot >> bit) % 2 == 0
                block = jnp.concatenate(
                    [jnp.where(low, block, other), jnp.where(low, other, block)], axis=0
                )
            return block

        def spread(line, meets=(0, 0)):
            line = traffic.meet(line, meets[0])
            posts = [post_plane(line, k) for k in range(1, row)]
            others = yield posts
            near = traffic.meet(jnp.concatenate([line, *others], axis=0), meets[1])
            (far,) = yield [post_core(near)]
            return jnp.concatenate([near, far], axis=0)

        def collect(partial, meets=1):
            half = partial.shape[0] // 2
            (other,) = yield [post_core(narrow(partial[half:]))]
            near = partial[:half] + wide(other)
            size = half // row
            sent = [narrow(near[k * size : (k + 1) * size]) for k in range(1, row)]
            posts = [post_plane(values, k) for k, values in enumerate(sent, 1)]
            others = yield posts
            line = near[:size]
            for other in others:
                line = line + wide(other)
            for bit in range(line_bits):
                sent = narrow(line)
                if bit == 1:
                    sent = traffic.meet(sent, meets)
                posts = [post_line(sent, bit)]
                (other,) = yield posts
                line = wide(sent) + wide(other)
            return line

        def squares(values):
            values = wide(values)
            return jnp.sum(values * values, axis=1, keepdims=True)

        def inverse_rms(total):
            return lax.rsqrt(total / width + eps)

        def far_grads():
            parts = jnp.concatenate([cotangent[r] for r in ranges], axis=1)
            line = yield from gather_line(parts)
            cots.extend(jnp.split(line, CHUNKS, axis=1))
            everywhere = yield from spread(line)
            for part in jnp.split(everywhere, CHUNKS, axis=1):
                partial = product(part, down2, 1)
                hidden_grads.append((partial, post_sum(partial)))
                yield None

        def chunk(i):
            resid = yield from gather_line(after(resid_in[ranges[i]], traffic.token))

            stream = yield from spread(resid, (0, i))
            scaled = narrow(wide(stream) * norm1_gain)
            gate = product(scaled, gate1)
            posts = [post_sum(gate)]
            up = product(scaled, up1)
            posts.append(post_sum(up))
            total = squares(stream)
            posts.append(post_sum(total, exact=True))
            gate_other, up_other, total_other = yield posts
            inv = inverse_rms(total + total_other)
            hidden = narrow(
                jax.nn.silu((gate + wide(gate_other)) * inv) * ((up + wide(up_other)) * inv)
            )
            block_out = yield from collect(product(hidden, down1))
            block_out = narrow(wide(resid) + block_out)
            home = narrow(wide(block_out) - dec_bias)

            centered = yield from spread(home, (1, 1))
            preact = product(centered, enc_weight)
            others = yield post_pieces(preact)
            preact = preact + wide(jnp.concatenate(others, axis=0)) + enc_bias
            slope = jax.nn.sigmoid(4.0 * preact)
            codes = narrow(jax.nn.softplus(4.0 * preact) / 4.0)
            recon = yield from collect(product(codes, dec_weight))
            recon = narrow(recon + dec_bias)

            stream = yield from spread(recon, (1, 1))
            scaled = narrow(wide(stream) * norm2_gain)
            gate = product(scaled, gate2)
            posts = [post_sum(gate)]
            up = product(scaled, up2)
            posts.append(post_sum(up))
            total = squares(stream)
            posts.append(post_sum(total, exact=True))
            hidden_grad, hidden_post = hidden_grads[i]
            gate_other, up_other, total_other, hidden_other = yield [*posts, hidden_post]
            inv = inverse_rms(total + total_other)
            gate, up = (gate + wide(gate_other)) * inv, (up + wide(up_other)) * inv
            hidden_grad = hidden_grad + wide(hidden_other)
            squash = jax.nn.sigmoid(gate)
            gate_grad = narrow(hidden_grad * up * squash * (1.0 + gate * (1.0 - squash)))
            up_grad = narrow(hidden_grad * gate * squash)
            normed_grad = yield from collect(
                product(gate_grad, gate2, 1) + product(up_grad, up2, 1), CHUNKS - 1 - i
            )
            scaled_grad = normed_grad * norm2_gain
            recon_f = wide(recon)
            inner = jnp.sum(scaled_grad * recon_f, axis=1, keepdims=True)
            inner_other = post_sum(inner, exact=True)
            inner = (inner + inner_other) / width
            inv = inv[: recon.shape[0]]
            home = narrow(wide(cots[i]) + scaled_grad * inv - recon_f * inv**3 * inner)

            recon_grad = yield from spread(home, (1, 1))
            codes_grad = product(recon_grad, dec_weight, 1)
            others = yield post_pieces(codes_grad)
            preact_grad = narrow((codes_grad + wide(jnp.concatenate(others, axis=0))) * slope)
            return codes, recon_grad, centered, preact_grad

        ranges = [slice(i * rows, (i + 1) * rows) for i in range(CHUNKS)]
        cots, hidden_grads = [], []
        parts = traffic.run({"a": chunk(0), "b": chunk(1), "c": far_grads()}, ORDER)
        parts = [parts["a"], parts["b"]]
        codes, recon_grad, centered, preact_grad = (
            jnp.concatenate(pieces, axis=0) for pieces in zip(*parts)
        )
        dec_grad = contract(codes, recon_grad, 0, 0)
        enc_grad = contract(centered, preact_grad, 0, 0)
        return (enc_grad, dec_grad)

    return on_device


def solution(mesh):
    in_specs = (
        P("latent", "mp"),
        P("latent", "mp"),
        P("mp"),
        P("mp", "latent"),
        P("mp", "latent"),
        P("latent", "mp"),
        P("mp", "latent"),
        P("latent"),
        P("latent", "mp"),
        P("mp"),
        P("mp"),
        P("mp", "latent"),
        P("mp", "latent"),
        P("latent", "mp"),
    )
    out_specs = (P("mp", "latent"), P("latent", "mp"))
    step = make_step(mesh.shape["mp"], mesh.shape["latent"])
    return jax.shard_map(step, mesh=mesh, in_specs=in_specs, out_specs=out_specs, check_vma=False)
```

```python
import jax
import jax.numpy as jnp
from jax import lax
from jax.sharding import PartitionSpec as P

CHUNKS = 2
ORDER = (
    ("aaacaca" + "bbb")
    + ("abab" + "acaa" + "bacbabcbb")
    + ("ababacaa" + "bababbb")
    + ("ababaaa" + "bababbb")
    + ("bb" + "ab")
)
FIRST_PIECE = 4


def matmul(left, right):
    return jnp.dot(left, right, preferred_element_type=jnp.float32)


def contract(left, right, left_dim, right_dim):
    return lax.dot_general(
        left, right, (((left_dim,), (right_dim,)), ((), ())), preferred_element_type=jnp.float32
    )


def narrow(values):
    return values.astype(jnp.bfloat16)


def wide(values):
    return values.astype(jnp.float32)


def swap(values, axis, size, mask):
    return lax.ppermute(values, axis, [(i, i ^ mask) for i in range(size)])


def after(values, token):
    width = values.shape[1]
    if token is None or width == 1:
        return values
    pieces = -(-width // token.shape[1])
    edge = jnp.concatenate([token[k : k + 1] for k in range(pieces)], axis=1)[:, :width]
    return jnp.where(edge == edge, values, jnp.zeros_like(values))


def beside(column, rows):
    rows = rows[:, :128]
    return column * jnp.max(jnp.where(rows == rows, 1.0, 0.0), axis=1, keepdims=True)


class Traffic:
    def __init__(self):
        self.token = None
        self.pending = []

    def post(self, values, axis, size, mask):
        self.token = values
        return swap(values, axis, size, mask)

    def post_sum(self, values, size):
        got = self.post(values, "mp", size, 1)
        self.pending.append(got)
        return got

    def meet(self, values, count=1):
        for got in self.pending[:count]:
            values = after(values, got)
        self.pending = self.pending[count:]
        return values

    def run(self, generators, order):
        held, results = {}, {}
        for name in order:
            values = held.get(name)
            if values is not None:
                values = [after(got, self.token) for got in values]
            try:
                held[name] = generators[name].send(values)
            except StopIteration as end:
                results[name] = end.value
        return results


def make_step(mp, latent):
    chips = latent // 2
    line_size = min(4, chips)
    row = chips // line_size
    line_bits = line_size.bit_length() - 1

    def on_device(
        resid_in,
        cotangent,
        norm1_gain,
        gate1,
        up1,
        down1,
        enc_weight,
        enc_bias,
        dec_weight,
        dec_bias,
        norm2_gain,
        gate2,
        up2,
        down2,
    ):
        eps = 1e-05
        width = resid_in.shape[1] * mp
        rows = resid_in.shape[0] // CHUNKS
        traffic = Traffic()

        def product(left, right, right_dim=0):
            return contract(left, right, 1, right_dim)

        def post_line(values, bit):
            return traffic.post(values, "latent", latent, 2 * row << bit)

        def post_plane(values, k):
            return traffic.post(values, "latent", latent, 2 * k)

        def post_core(values):
            return traffic.post(values, "latent", latent, 1)

        def post_sum(partial, exact=False):
            if mp != 2:
                return lax.psum(wide(partial), "mp") - wide(partial)
            if exact:
                return swap(partial, "mp", mp, 1)
            return traffic.post_sum(partial, mp)

        def post_pieces(partial):
            first = partial.shape[0] // FIRST_PIECE
            return [post_sum(partial[:first]), post_sum(partial[first:])]

        def gather_line(block):
            spot = (lax.axis_index("latent") // (2 * row)) % line_size
            for bit in range(line_bits):
                (other,) = yield [post_line(block, bit)]
                low = (spot >> bit) % 2 == 0
                block = jnp.concatenate(
                    [jnp.where(low, block, other), jnp.where(low, other, block)], axis=0
                )
            return block

        def spread(line, meets=(0, 0)):
            line = traffic.meet(line, meets[0])
            posts = [post_plane(line, k) for k in range(1, row)]
            others = yield posts
            near = traffic.meet(jnp.concatenate([line, *others], axis=0), meets[1])
            (far,) = yield [post_core(near)]
            return jnp.concatenate([near, far], axis=0)

        def collect(partial, meets=1):
            half = partial.shape[0] // 2
            (other,) = yield [post_core(narrow(partial[half:]))]
            near = partial[:half] + wide(other)
            size = half // row
            sent = [narrow(near[k * size : (k + 1) * size]) for k in range(1, row)]
            posts = [post_plane(values, k) for k, values in enumerate(sent, 1)]
            others = yield posts
            line = near[:size]
            for other in others:
                line = line + wide(other)
            for bit in range(line_bits):
                sent = narrow(line)
                if bit == 1:
                    sent = traffic.meet(sent, meets)
                posts = [post_line(sent, bit)]
                (other,) = yield posts
                line = wide(sent) + wide(other)
            return line

        def squares(values):
            values = wide(values)
            return jnp.sum(values * values, axis=1, keepdims=True)

        def inverse_rms(total):
            return lax.rsqrt(total / width + eps)

        def far_grads():
            parts = jnp.concatenate([cotangent[r] for r in ranges], axis=1)
            line = yield from gather_line(parts)
            cots.extend(jnp.split(line, CHUNKS, axis=1))
            everywhere = yield from spread(line)
            for part in jnp.split(everywhere, CHUNKS, axis=1):
                partial = narrow(product(part, down2, 1))
                hidden_grads.append((partial, post_sum(partial)))
                yield None

        def chunk(i):
            resid = yield from gather_line(after(resid_in[ranges[i]], traffic.token))

            stream = yield from spread(resid, (0, i))
            scaled = narrow(wide(stream) * norm1_gain)
            gate = narrow(product(scaled, gate1))
            posts = [post_sum(gate)]
            up = narrow(product(scaled, up1))
            token = traffic.token
            posts.append(post_sum(after(up, posts[0])))
            traffic.token = token
            total = squares(stream)
            posts.append(post_sum(total, exact=True))
            gate_other, up_other, total_other = yield posts
            inv = inverse_rms(total + beside(total_other, up_other))
            hidden = narrow(
                jax.nn.silu((wide(gate) + wide(gate_other)) * inv)
                * ((wide(up) + wide(up_other)) * inv)
            )
            block_out = yield from collect(product(hidden, down1))
            block_out = narrow(wide(resid) + block_out)
            home = narrow(wide(block_out) - dec_bias)

            centered = yield from spread(home, (1, 1))
            preact = narrow(product(centered, enc_weight))
            others = yield post_pieces(preact)
            preact = wide(preact) + wide(jnp.concatenate(others, axis=0)) + enc_bias
            slope = narrow(jax.nn.sigmoid(4.0 * preact))
            codes = narrow(jax.nn.softplus(4.0 * preact) / 4.0)
            recon = yield from collect(product(codes, dec_weight))
            recon = narrow(recon + dec_bias)

            stream = yield from spread(recon, (1, 1))
            scaled = narrow(wide(stream) * norm2_gain)
            gate = narrow(product(scaled, gate2))
            posts = [post_sum(gate)]
            up = narrow(product(scaled, up2))
            token = traffic.token
            posts.append(post_sum(after(up, posts[0])))
            traffic.token = token
            total = squares(stream)
            posts.append(post_sum(total, exact=True))
            hidden_grad, hidden_post = hidden_grads[i]
            gate_other, up_other, total_other, hidden_other = yield [*posts, hidden_post]
            inv = inverse_rms(total + beside(total_other, up_other))
            gate = (wide(gate) + wide(gate_other)) * inv
            up = (wide(up) + wide(up_other)) * inv
            hidden_grad = wide(hidden_grad) + wide(hidden_other)
            squash = jax.nn.sigmoid(gate)
            hidden_grad = hidden_grad * inv
            gate_grad = narrow(hidden_grad * up * squash * (1.0 + gate * (1.0 - squash)))
            up_grad = narrow(hidden_grad * gate * squash)
            partial = product(gate_grad, gate2, 1) + product(up_grad, up2, 1)
            inner = jnp.sum(wide(gate_grad) * gate + wide(up_grad) * up, axis=1, keepdims=True) * inv
            inner = jnp.broadcast_to(inner, (inner.shape[0], 128))
            sums = yield from collect(jnp.concatenate([partial, inner], axis=1), CHUNKS - 1 - i)
            inner = sums[:, -1:] / width
            home = narrow(wide(cots[i]) + sums[:, :-128] * norm2_gain - wide(recon) * inner)

            recon_grad = yield from spread(home, (1, 1))
            codes_grad = narrow(product(recon_grad, dec_weight, 1))
            others = yield post_pieces(codes_grad)
            preact_grad = narrow((wide(codes_grad) + wide(jnp.concatenate(others, axis=0))) * wide(slope))
            return codes, recon_grad, centered, preact_grad

        ranges = [slice(i * rows, (i + 1) * rows) for i in range(CHUNKS)]
        cots, hidden_grads = [], []
        parts = traffic.run({"a": chunk(0), "b": chunk(1), "c": far_grads()}, ORDER)
        parts = [parts["a"], parts["b"]]
        codes, recon_grad, centered, preact_grad = (
            jnp.concatenate(pieces, axis=0) for pieces in zip(*parts)
        )
        dec_grad = contract(codes, recon_grad, 0, 0)
        enc_grad = contract(centered, preact_grad, 0, 0)
        return (enc_grad, dec_grad)

    return on_device


def solution(mesh):
    in_specs = (
        P("latent", "mp"),
        P("latent", "mp"),
        P("mp"),
        P("mp", "latent"),
        P("mp", "latent"),
        P("latent", "mp"),
        P("mp", "latent"),
        P("latent"),
        P("latent", "mp"),
        P("mp"),
        P("mp"),
        P("mp", "latent"),
        P("mp", "latent"),
        P("latent", "mp"),
    )
    out_specs = (P("mp", "latent"), P("latent", "mp"))
    step = make_step(mesh.shape["mp"], mesh.shape["latent"])
    return jax.shard_map(step, mesh=mesh, in_specs=in_specs, out_specs=out_specs, check_vma=False)
```

```python
import jax
import jax.numpy as jnp
from jax import lax
from jax.sharding import PartitionSpec as P

CHUNKS = 2
ORDER = (
    ("aaacaa" + "bbcb")
    + ("abab" + "acaa" + "bacbabcbb")
    + ("ababacaa" + "bababbb")
    + ("ababaaa" + "bababbb")
    + ("bb" + "ab")
)
FIRST_PIECE = 4


def matmul(left, right):
    return jnp.dot(left, right, preferred_element_type=jnp.float32)


def contract(left, right, left_dim, right_dim):
    return lax.dot_general(
        left, right, (((left_dim,), (right_dim,)), ((), ())), preferred_element_type=jnp.float32
    )


def narrow(values):
    return values.astype(jnp.bfloat16)


def wide(values):
    return values.astype(jnp.float32)


def swap(values, axis, size, mask):
    return lax.ppermute(values, axis, [(i, i ^ mask) for i in range(size)])


def after(values, token):
    width = values.shape[1]
    if token is None or width == 1:
        return values
    pieces = -(-width // token.shape[1])
    edge = jnp.concatenate([token[k : k + 1] for k in range(pieces)], axis=1)[:, :width]
    return jnp.where(edge == edge, values, jnp.zeros_like(values))


def beside(column, rows):
    rows = rows[:, :128]
    return column * jnp.max(jnp.where(rows == rows, 1.0, 0.0), axis=1, keepdims=True)


class Traffic:
    def __init__(self):
        self.token = None
        self.pending = []

    def post(self, values, axis, size, mask):
        self.token = values
        return swap(values, axis, size, mask)

    def post_sum(self, values, size):
        got = self.post(values, "mp", size, 1)
        self.pending.append(got)
        return got

    def meet(self, values, count=1):
        for got in self.pending[:count]:
            values = after(values, got)
        self.pending = self.pending[count:]
        return values

    def run(self, generators, order):
        held, results = {}, {}
        for name in order:
            values = held.get(name)
            if values is not None:
                values = [after(got, self.token) for got in values]
            try:
                held[name] = generators[name].send(values)
            except StopIteration as end:
                results[name] = end.value
        return results


def make_step(mp, latent):
    chips = latent // 2
    line_size = min(4, chips)
    row = chips // line_size
    line_bits = line_size.bit_length() - 1

    def on_device(
        resid_in,
        cotangent,
        norm1_gain,
        gate1,
        up1,
        down1,
        enc_weight,
        enc_bias,
        dec_weight,
        dec_bias,
        norm2_gain,
        gate2,
        up2,
        down2,
    ):
        eps = 1e-05
        width = resid_in.shape[1] * mp
        rows = resid_in.shape[0] // CHUNKS
        traffic = Traffic()

        def product(left, right, right_dim=0):
            return contract(left, right, 1, right_dim)

        def post_line(values, bit):
            return traffic.post(values, "latent", latent, 2 * row << bit)

        def post_plane(values, k):
            return traffic.post(values, "latent", latent, 2 * k)

        def post_core(values):
            return traffic.post(values, "latent", latent, 1)

        def post_sum(partial, exact=False):
            if mp != 2:
                return lax.psum(wide(partial), "mp") - wide(partial)
            if exact:
                return swap(partial, "mp", mp, 1)
            return traffic.post_sum(partial, mp)

        def post_pieces(partial):
            first = partial.shape[0] // FIRST_PIECE
            return [post_sum(partial[:first]), post_sum(partial[first:])]

        def gather_line(block):
            spot = (lax.axis_index("latent") // (2 * row)) % line_size
            for bit in range(line_bits):
                (other,) = yield [post_line(block, bit)]
                low = (spot >> bit) % 2 == 0
                block = jnp.concatenate(
                    [jnp.where(low, block, other), jnp.where(low, other, block)], axis=0
                )
            return block

        def spread(line, meets=(0, 0)):
            line = traffic.meet(line, meets[0])
            posts = [post_plane(line, k) for k in range(1, row)]
            others = yield posts
            near = traffic.meet(jnp.concatenate([line, *others], axis=0), meets[1])
            (far,) = yield [post_core(near)]
            return jnp.concatenate([near, far], axis=0)

        def collect(partial, meets=1):
            half = partial.shape[0] // 2
            (other,) = yield [post_core(narrow(partial[half:]))]
            near = partial[:half] + wide(other)
            size = half // row
            sent = [narrow(near[k * size : (k + 1) * size]) for k in range(1, row)]
            posts = [post_plane(values, k) for k, values in enumerate(sent, 1)]
            others = yield posts
            line = near[:size]
            for other in others:
                line = line + wide(other)
            for bit in range(line_bits):
                sent = narrow(line)
                if bit == 1:
                    sent = traffic.meet(sent, meets)
                posts = [post_line(sent, bit)]
                (other,) = yield posts
                line = wide(sent) + wide(other)
            return line

        def squares(values):
            values = wide(values)
            return jnp.sum(values * values, axis=1, keepdims=True)

        def inverse_rms(total):
            return lax.rsqrt(total / width + eps)

        def far_grads():
            parts = jnp.concatenate([cotangent[r] for r in ranges], axis=1)
            line = yield from gather_line(parts)
            cots.extend(jnp.split(line, CHUNKS, axis=1))
            everywhere = yield from spread(line)
            for part in jnp.split(everywhere, CHUNKS, axis=1):
                partial = narrow(product(part, down2, 1))
                hidden_grads.append((partial, post_sum(partial)))
                yield None

        def chunk(i):
            resid = yield from gather_line(after(resid_in[ranges[i]], traffic.token))

            stream = yield from spread(resid, (0, i))
            scaled = narrow(wide(stream) * norm1_gain)
            gate = narrow(product(scaled, gate1))
            posts = [post_sum(gate)]
            up = narrow(product(scaled, up1))
            token = traffic.token
            posts.append(post_sum(after(up, posts[0]) if i else up))
            traffic.token = token
            total = squares(stream)
            posts.append(post_sum(total, exact=True))
            gate_other, up_other, total_other = yield posts
            inv = inverse_rms(total + beside(total_other, up_other))
            hidden = narrow(
                jax.nn.silu((wide(gate) + wide(gate_other)) * inv)
                * ((wide(up) + wide(up_other)) * inv)
            )
            block_out = yield from collect(product(hidden, down1))
            block_out = narrow(wide(resid) + block_out)
            home = narrow(wide(block_out) - dec_bias)

            centered = yield from spread(home, (1, 1))
            preact = narrow(product(centered, enc_weight))
            others = yield post_pieces(preact)
            preact = wide(preact) + wide(jnp.concatenate(others, axis=0)) + enc_bias
            slope = narrow(jax.nn.sigmoid(4.0 * preact))
            codes = narrow(jax.nn.softplus(4.0 * preact) / 4.0)
            recon = yield from collect(product(codes, dec_weight))
            recon = narrow(recon + dec_bias)

            stream = yield from spread(recon, (1, 1))
            scaled = narrow(wide(stream) * norm2_gain)
            gate = narrow(product(scaled, gate2))
            posts = [post_sum(gate)]
            up = narrow(product(scaled, up2))
            token = traffic.token
            posts.append(post_sum(after(up, posts[0])))
            traffic.token = token
            total = squares(stream)
            posts.append(post_sum(total, exact=True))
            hidden_grad, hidden_post = hidden_grads[i]
            gate_other, up_other, total_other, hidden_other = yield [*posts, hidden_post]
            inv = inverse_rms(total + beside(total_other, up_other))
            gate = (wide(gate) + wide(gate_other)) * inv
            up = (wide(up) + wide(up_other)) * inv
            hidden_grad = wide(hidden_grad) + wide(hidden_other)
            squash = jax.nn.sigmoid(gate)
            hidden_grad = hidden_grad * inv
            gate_grad = narrow(hidden_grad * up * squash * (1.0 + gate * (1.0 - squash)))
            up_grad = narrow(hidden_grad * gate * squash)
            partial = product(gate_grad, gate2, 1) + product(up_grad, up2, 1)
            inner = jnp.sum(wide(gate_grad) * gate + wide(up_grad) * up, axis=1, keepdims=True) * inv
            inner = jnp.broadcast_to(inner, (inner.shape[0], 128))
            sums = yield from collect(jnp.concatenate([partial, inner], axis=1), CHUNKS - 1 - i)
            inner = sums[:, -1:] / width
            home = narrow(wide(cots[i]) + sums[:, :-128] * norm2_gain - wide(recon) * inner)

            recon_grad = yield from spread(home, (1, 1))
            codes_grad = narrow(product(recon_grad, dec_weight, 1))
            others = yield post_pieces(codes_grad)
            preact_grad = narrow((wide(codes_grad) + wide(jnp.concatenate(others, axis=0))) * wide(slope))
            return codes, recon_grad, centered, preact_grad

        ranges = [slice(i * rows, (i + 1) * rows) for i in range(CHUNKS)]
        cots, hidden_grads = [], []
        parts = traffic.run({"a": chunk(0), "b": chunk(1), "c": far_grads()}, ORDER)
        parts = [parts["a"], parts["b"]]
        codes, recon_grad, centered, preact_grad = (
            jnp.concatenate(pieces, axis=0) for pieces in zip(*parts)
        )
        dec_grad = contract(codes, recon_grad, 0, 0)
        enc_grad = contract(centered, preact_grad, 0, 0)
        return (enc_grad, dec_grad)

    return on_device


def solution(mesh):
    in_specs = (
        P("latent", "mp"),
        P("latent", "mp"),
        P("mp"),
        P("mp", "latent"),
        P("mp", "latent"),
        P("latent", "mp"),
        P("mp", "latent"),
        P("latent"),
        P("latent", "mp"),
        P("mp"),
        P("mp"),
        P("mp", "latent"),
        P("mp", "latent"),
        P("latent", "mp"),
    )
    out_specs = (P("mp", "latent"), P("latent", "mp"))
    step = make_step(mesh.shape["mp"], mesh.shape["latent"])
    return jax.shard_map(step, mesh=mesh, in_specs=in_specs, out_specs=out_specs, check_vma=False)
```
